32 devices in a mesh: group: 2 (over x), narrow: 16 (over z, y, core).
Axes of the slice: x: 2, y: 2, z: 4, core: 2. Of those that a mesh axis runs over, the one named last changes fastest.
Arguments:
- prefill_rows: bfloat16 [32, 6144], P(('group', 'narrow')), parts along dimension 0, may hold values from -6 to 6
- decode_rows: bfloat16 [32, 3, 6144], P(('group', 'narrow')), parts along dimension 0, may hold values from -6 to 6
- kv_cache: bfloat16 [32, 2048, 256], P(('group', 'narrow')), parts along dimension 0, may hold values from -300 to 300, as said below
- slot_lengths: int32 [32], P(('group', 'narrow')), parts along dimension 0, may hold values from 1 to 2048
- prefill_slot: int32 [2], P('group'), parts along dimension 0, may hold values from 0 to 15
- norm_gain: float32 [6144], replicated, may hold values from 0.1 to 1.9
- query_weight: bfloat16 [6144, 6144], P(None, 'narrow'), may hold values from -0.1875 to 0.1875
- keyval_weight: bfloat16 [6144, 256], P('narrow'), may hold values from -0.078125 to 0.078125
- output_weight: bfloat16 [6144, 6144], P('narrow'), may hold values from -0.21875 to 0.21875
Outputs:
- prefill_out: bfloat16 [32, 6144], P(('group', 'narrow')), parts along dimension 0
- decode_out: bfloat16 [32, 3, 6144], P(('group', 'narrow')), parts along dimension 0
The draws below stay inside these ranges and needn't reach their ends.
There are 2 independent parts, one for each index of `group`. The reference program is written for one: setup_inputs(seed, part) draws one part's arguments, and reference() takes and returns one part's arrays. A program takes and returns all parts, laid end to end along the dimension named above; an argument that names none is the same for every part. Nothing has to cross between parts.
Inputs may be any that keep to these rules, and one draw needn't show every extreme that they name: `kv_cache`: entries are of order one in the values; key entries may be far larger.
All inputs are finite; a program needn't handle non-finite values.
Results may differ from the reference program's by a relative error of at most 0.0075.
The reference program's roundings to bfloat16 on the way count: a program that leaves them out, or rounds other values in their place, can miss the bound.
Values may be sent and summed in bfloat16 or wider, within the bound.
A program may use at most 64 MiB of HBM per device.

```python
import jax
import jax.numpy as jnp
from jax import lax

D = 6144
HEADS = 48
HEAD_DIM = 128
CACHE = 2048
STEPS = 3
SLOTS = 16
PREFILL = 16


def draw_kv_cache(key, part):
    first_key = jax.random.fold_in(jax.random.fold_in(key, 17), 0)
    base = jax.random.normal(first_key, (SLOTS, CACHE, 2 * HEAD_DIM), jnp.float32)
    base = jnp.clip(base, -5.0, 5.0)
    return base.astype(jnp.bfloat16)


def touch_ends(entries, rng, low, high):
    dims = entries.shape
    place = [jax.random.randint(jax.random.fold_in(rng, axis), (), 0, dims[axis]) for axis in range(len(dims))]
    entries = entries.at[tuple(place)].set(low)
    longest = dims.index(max(dims))
    place[longest] = (place[longest] + 1) % dims[longest]
    return entries.at[tuple(place)].set(high)


def levels(stream_key, dims, cuts, smallest, top_value):
    loudness, own = 1.0, jax.random.fold_in(stream_key, 6)
    for dim, blocks in cuts:
        draws = jnp.exp(jax.random.uniform(jax.random.fold_in(own, dim), (blocks,), jnp.float32, smallest / len(cuts), top_value / len(cuts)))
        loudness = loudness * jnp.repeat(draws, dims[dim] // blocks).reshape([-1 if axis == dim else 1 for axis in range(len(dims))])
    return loudness


def normal_values(key, dims, scale, reach, pieces=(), kind=jnp.bfloat16):
    result = scale * jax.random.normal(key, dims, jnp.float32)
    if pieces:
        result = result * levels(key, dims, pieces, -0.22, 0.18)
    return jnp.clip(result, -reach, reach).astype(kind)


def setup_inputs(seed: int = 0, part: int = 0) -> dict:
    streams_of = jax.random.split(jax.random.key(seed), 10)
    part_keys = jax.random.split(jax.random.fold_in(streams_of[9], part), 10)
    return {
        "prefill_rows": normal_values(part_keys[0], (PREFILL, D), 1.0, 6.0, ((0, 16),)),
        "decode_rows": normal_values(part_keys[1], (SLOTS, STEPS, D), 1.0, 6.0, ((0, 16),)),
        "kv_cache": draw_kv_cache(jax.random.fold_in(jax.random.fold_in(streams_of[9], part), 71), part),
        "slot_lengths": touch_ends(jax.random.randint(part_keys[3], (SLOTS,), 1, CACHE + 1), jax.random.fold_in(part_keys[3], 1), 1, CACHE).astype(jnp.int32),
        "prefill_slot": jax.random.randint(part_keys[4], (1,), 0, SLOTS).astype(jnp.int32),
        "norm_gain": jnp.clip(1.0 + 0.18 * jax.random.normal(streams_of[5], (D,), jnp.float32), 0.1, 1.9),
        "query_weight": normal_values(streams_of[6], (D, HEADS * HEAD_DIM), (D // 6) ** -0.5, 0.1875, ((1, 16),)),
        "keyval_weight": normal_values(streams_of[7], (D, 2 * HEAD_DIM), D ** -0.5, 0.078125, ((0, 16),)),
        "output_weight": normal_values(streams_of[8], (HEADS * HEAD_DIM, D), (D // 9) ** -0.5, 0.21875, ((0, 16),)),
    }


EPSILON = 1e-05

def layer_norm(inputs, gain):
    values = inputs.astype(jnp.float32)
    center = values - lax.optimization_barrier(jnp.mean(values, axis=-1, keepdims=True))
    spread = lax.optimization_barrier(jnp.mean(center * center, axis=-1, keepdims=True))
    return (center * lax.rsqrt(spread + EPSILON) * gain).astype(jnp.bfloat16)

def attend(queries, keyvals, allowed):
    keys = keyvals[:, :HEAD_DIM].astype(jnp.float32)
    values = keyvals[:, HEAD_DIM:].astype(jnp.float32)
    scores = jnp.einsum('rhd,kd->rhk', queries.astype(jnp.float32), keys) * HEAD_DIM ** (-0.5)
    masked = jnp.where(allowed, scores, -1e+30)
    highest = lax.optimization_barrier(jnp.max(masked, axis=-1, keepdims=True))
    weights = jnp.where(allowed, jnp.exp(scores - highest), 0.0)
    total = lax.optimization_barrier(jnp.sum(weights, axis=-1))
    rounded = lax.optimization_barrier(weights.astype(jnp.bfloat16)).astype(jnp.float32)
    mixed = jnp.einsum('rhk,kd->rhd', rounded, values)
    return mixed / total[..., None]

def reference(prefill_rows, decode_rows, kv_cache, slot_lengths, prefill_slot, norm_gain, query_weight, keyval_weight, output_weight):
    width = HEADS * HEAD_DIM
    normed = layer_norm(prefill_rows, norm_gain)
    queries = jnp.dot(normed, query_weight, preferred_element_type=jnp.float32).astype(jnp.bfloat16)
    queries = queries.reshape(PREFILL, HEADS, HEAD_DIM)
    keyvals = jnp.dot(normed, keyval_weight, preferred_element_type=jnp.float32).astype(jnp.bfloat16)
    position = jnp.arange(PREFILL, dtype=jnp.int32)
    allowed = (position[None, :] <= position[:, None])[:, None, :]
    mixed = attend(queries, keyvals, allowed).astype(jnp.bfloat16).reshape(PREFILL, width)
    prefill_out = jnp.dot(mixed, output_weight, preferred_element_type=jnp.float32).astype(jnp.bfloat16)
    dec_normed = layer_norm(decode_rows, norm_gain).reshape(SLOTS * STEPS, D)
    dec_queries = jnp.dot(dec_normed, query_weight, preferred_element_type=jnp.float32).astype(jnp.bfloat16)
    dec_queries = dec_queries.reshape(SLOTS, STEPS, HEADS, HEAD_DIM)
    fresh = jnp.dot(dec_normed, keyval_weight, preferred_element_type=jnp.float32).astype(jnp.bfloat16)
    fresh = fresh.reshape(SLOTS, STEPS, 2 * HEAD_DIM)
    slot_ids = jnp.arange(SLOTS, dtype=jnp.int32)
    chosen = slot_ids == prefill_slot[0]
    live_length = jnp.where(chosen, PREFILL, slot_lengths).astype(jnp.int32)
    padded_prefill = jnp.concatenate([keyvals, jnp.zeros((CACHE - PREFILL, 2 * HEAD_DIM), jnp.bfloat16)], axis=0)
    cache_pos = jnp.arange(CACHE, dtype=jnp.int32)
    step_pos = jnp.arange(STEPS, dtype=jnp.int32)
    step_mask = step_pos[None, :] <= step_pos[:, None]

    def per_slot(items):
        slot_queries, slot_fresh, slot_cache, slot_length, slot_chosen = items
        replace = jnp.logical_and(slot_chosen, cache_pos < PREFILL)[:, None]
        rows = jnp.where(replace, padded_prefill, slot_cache)
        every_row = jnp.concatenate([rows, slot_fresh], axis=0)
        cache_mask = jnp.broadcast_to((cache_pos < slot_length)[None, :], (STEPS, CACHE))
        allowed_rows = jnp.concatenate([cache_mask, step_mask], axis=1)[:, None, :]
        return attend(slot_queries, every_row, allowed_rows).astype(jnp.bfloat16)
    dec_mixed = lax.map(per_slot, (dec_queries, fresh, kv_cache, live_length, chosen))
    dec_mixed = dec_mixed.reshape(SLOTS * STEPS, width)
    decode_out = jnp.dot(dec_mixed, output_weight, preferred_element_type=jnp.float32)
    decode_out = decode_out.reshape(SLOTS, STEPS, D).astype(jnp.bfloat16)
    return (prefill_out, decode_out)
```

```python
import functools

import jax
import jax.numpy as jnp
from jax import lax
from jax.experimental import pallas as pl
from jax.experimental.pallas import tpu as pltpu
from jax.sharding import PartitionSpec as P

HEAD_DIM = 128
EPSILON = 1e-05
MESH = pl.DeviceIdType.MESH
VMEM = pl.BlockSpec(memory_space=pltpu.VMEM)
SMEM = pl.BlockSpec(memory_space=pltpu.SMEM)
LIMIT = 40 * 1024 * 1024


def greet(n, me):
    barrier = pltpu.get_barrier_semaphore()

    def hello(k, carry):
        peer = lax.rem(me + k, n)
        pl.semaphore_signal(barrier, inc=1, device_id={"narrow": peer}, device_id_type=MESH)
        return carry

    lax.fori_loop(1, n, hello, 0)
    return barrier


def remote(src, dst, send, recv, peer):
    return pltpu.make_async_remote_copy(
        src_ref=src,
        dst_ref=dst,
        send_sem=send,
        recv_sem=recv,
        device_id={"narrow": peer},
        device_id_type=MESH,
    )


def each(start, stop, body):
    def step(k, carry):
        body(k)
        return carry

    lax.fori_loop(start, stop, step, 0)


def gather_kernel(n, x_ref, gain_ref, out_ref, own, send, recv, fsend, frecv, local):
    me = lax.axis_index("narrow")
    core = lax.rem(me, 2)
    chip = me // 2
    chips = n // 2
    sibling = me + 1 - 2 * core
    barrier = greet(n, me)
    values = x_ref[...].astype(jnp.float32)
    center = values - jnp.mean(values, axis=-1, keepdims=True)
    spread = jnp.mean(center * center, axis=-1, keepdims=True)
    own[...] = (center * lax.rsqrt(spread + EPSILON) * gain_ref[...]).astype(jnp.bfloat16)
    pl.semaphore_wait(barrier, n - 1)

    def across(k):
        to = lax.rem(chip + k, chips) * 2 + core
        return remote(own, out_ref.at[me], send.at[k], recv.at[k], to)

    def arrived(k):
        return lax.rem(chip - k + chips, chips) * 2 + core

    def forward(k):
        src = arrived(k)
        return remote(out_ref.at[src], out_ref.at[src], fsend.at[k], frecv.at[k], sibling)

    each(1, chips, lambda k: across(k).start())
    first = remote(own, out_ref.at[me], fsend.at[0], frecv.at[0], sibling)
    first.start()
    keep = pltpu.make_async_copy(own, out_ref.at[me], local)
    keep.start()

    def relay(k):
        src = arrived(k)
        remote(own, out_ref.at[src], send.at[k], recv.at[k], sibling).wait_recv()
        forward(k).start()

    each(1, chips, relay)
    keep.wait()

    def finish(k):
        src = lax.rem(chip - k + chips, chips) * 2 + 1 - core
        remote(own, out_ref.at[src], fsend.at[k], frecv.at[k], sibling).wait_recv()

    each(0, chips, finish)
    first.wait_send()
    each(1, chips, lambda k: across(k).wait_send())
    each(1, chips, lambda k: forward(k).wait_send())


def gather_rows(n, rows, gain):
    height, width = rows.shape
    dma = pltpu.SemaphoreType.DMA
    return pl.pallas_call(
        functools.partial(gather_kernel, n),
        out_shape=jax.ShapeDtypeStruct((n, height, width), jnp.bfloat16),
        in_specs=[VMEM, VMEM],
        out_specs=VMEM,
        scratch_shapes=[
            pltpu.VMEM((height, width), jnp.bfloat16),
            dma((n // 2,)),
            dma((n // 2,)),
            dma((n // 2,)),
            dma((n // 2,)),
            dma,
        ],
        compiler_params=pltpu.CompilerParams(
            collective_id=0, has_side_effects=True, vmem_limit_bytes=LIMIT
        ),
    )(rows, gain)


def spread_out(n, me, src, dst, send, recv, local):
    def copy(k):
        peer = lax.rem(me + k, n)
        return remote(src.at[peer], dst.at[me], send.at[k], recv.at[k], peer)

    each(1, n, lambda k: copy(k).start())
    keep = pltpu.make_async_copy(src.at[me], dst.at[me], local)
    keep.start()

    def finish():
        keep.wait()

        def take(k):
            peer = lax.rem(me - k + n, n)
            remote(src.at[peer], dst.at[peer], send.at[k], recv.at[k], peer).wait_recv()

        each(1, n, take)
        each(1, n, lambda k: copy(k).wait_send())

    return finish


def query_kernel(
    n, q_ref, kv_ref, qout_ref, kvout_ref, parts, own, qs, qr, ks, kr, bs, br, local
):
    me = lax.axis_index("narrow")
    barrier = greet(n, me)
    pl.semaphore_wait(barrier, n - 1)
    finish_kv = spread_out(n, me, kv_ref, parts, ks, kr, local.at[0])
    finish_q = spread_out(n, me, q_ref, qout_ref, qs, qr, local.at[1])
    finish_kv()
    own[...] = jnp.sum(parts[...], axis=0).astype(jnp.bfloat16)

    def copy(k):
        peer = lax.rem(me + k, n)
        return remote(own, kvout_ref.at[me], bs.at[k], br.at[k], peer)

    each(1, n, lambda k: copy(k).start())
    keep = pltpu.make_async_copy(own, kvout_ref.at[me], local.at[2])
    keep.start()
    finish_q()
    keep.wait()

    def take(k):
        peer = lax.rem(me - k + n, n)
        remote(own, kvout_ref.at[peer], bs.at[k], br.at[k], peer).wait_recv()

    each(1, n, take)
    each(1, n, lambda k: copy(k).wait_send())


def exchange_queries(n, queries, partial):
    dma = pltpu.SemaphoreType.DMA
    return pl.pallas_call(
        functools.partial(query_kernel, n),
        out_shape=(
            jax.ShapeDtypeStruct(queries.shape, jnp.bfloat16),
            jax.ShapeDtypeStruct(partial.shape, jnp.bfloat16),
        ),
        in_specs=[VMEM, VMEM],
        out_specs=(VMEM, VMEM),
        scratch_shapes=[
            pltpu.VMEM(partial.shape, jnp.float32),
            pltpu.VMEM(partial.shape[1:], jnp.bfloat16),
        ]
        + [dma((n,))] * 6
        + [dma((3,))],
        compiler_params=pltpu.CompilerParams(
            collective_id=1, has_side_effects=True, vmem_limit_bytes=LIMIT
        ),
    )(queries, partial)


def attend_kernel(steps, height, local_heads, info_ref, q_ref, cache_ref, new_ref, out_ref):
    live, chosen, me = info_ref[0], info_ref[1], info_ref[2]
    queries = q_ref[...]
    count = queries.shape[0]
    scale = HEAD_DIM ** (-0.5)

    def scores_of(ref):
        return scale * lax.dot_general(
            queries,
            ref[:, :HEAD_DIM],
            (((1,), (1,)), ((), ())),
            preferred_element_type=jnp.float32,
        )

    row = lax.broadcasted_iota(jnp.int32, (count, 1), 0)
    token = lax.rem(row, height * local_heads) // local_heads
    limit = jnp.where(token < steps, live, 0)
    depth = cache_ref.shape[0]
    position = lax.broadcasted_iota(jnp.int32, (count, depth), 1)
    old = jnp.where(position < limit, scores_of(cache_ref), -1e30)
    fresh_count = new_ref.shape[0]
    column = lax.broadcasted_iota(jnp.int32, (count, fresh_count), 1)
    owner = column // height
    kind = lax.rem(column, height)
    reach = jnp.where(token < steps, jnp.where(chosen > 0, fresh_count, -1), me)
    from_prefill = (kind == steps) & (owner <= reach)
    from_steps = (kind < steps) & (kind <= token) & (token < steps) & (owner == me)
    new = jnp.where(from_prefill | from_steps, scores_of(new_ref), -1e30)
    highest = jnp.maximum(
        jnp.max(old, axis=-1, keepdims=True), jnp.max(new, axis=-1, keepdims=True)
    )
    old = jnp.exp(old - highest)
    new = jnp.exp(new - highest)
    total = jnp.sum(old, axis=-1, keepdims=True) + jnp.sum(new, axis=-1, keepdims=True)
    mixed = jnp.dot(
        old.astype(jnp.bfloat16), cache_ref[:, HEAD_DIM:], preferred_element_type=jnp.float32
    )
    mixed = mixed + jnp.dot(
        new.astype(jnp.bfloat16), new_ref[:, HEAD_DIM:], preferred_element_type=jnp.float32
    )
    out_ref[...] = (mixed / total).astype(jnp.bfloat16)


def attend(steps, height, local_heads, info, queries, cache, new):
    return pl.pallas_call(
        functools.partial(attend_kernel, steps, height, local_heads),
        out_shape=jax.ShapeDtypeStruct(queries.shape, jnp.bfloat16),
        in_specs=[SMEM, VMEM, VMEM, VMEM],
        out_specs=VMEM,
        compiler_params=pltpu.CompilerParams(vmem_limit_bytes=LIMIT),
    )(info, queries, cache, new)


def mixed_kernel(n, x_ref, out_ref, send, recv, local):
    me = lax.axis_index("narrow")
    barrier = greet(n, me)
    pl.semaphore_wait(barrier, n - 1)
    spread_out(n, me, x_ref, out_ref, send, recv, local)()


def exchange_mixed(n, mixed):
    dma = pltpu.SemaphoreType.DMA
    return pl.pallas_call(
        functools.partial(mixed_kernel, n),
        out_shape=jax.ShapeDtypeStruct(mixed.shape, mixed.dtype),
        in_specs=[VMEM],
        out_specs=VMEM,
        scratch_shapes=[dma((n,)), dma((n,)), dma],
        compiler_params=pltpu.CompilerParams(
            collective_id=2, has_side_effects=True, vmem_limit_bytes=LIMIT
        ),
    )(mixed)


def reduce_kernel(n, x_ref, out_ref, near, pair, far, psend, precv, send, recv):
    me = lax.axis_index("narrow")
    core = lax.rem(me, 2)
    chip = me // 2
    chips = n // 2
    sibling = me + 1 - 2 * core
    barrier = greet(n, me)
    pl.semaphore_wait(barrier, n - 1)

    def target(k):
        return lax.rem(chip + k, chips)

    def swap(k):
        return remote(
            x_ref.at[target(k) * 2 + 1 - core],
            near.at[k],
            psend.at[k],
            precv.at[k],
            sibling,
        )

    def across(k):
        return remote(
            pair.at[k], far.at[k], send.at[k], recv.at[k], target(k) * 2 + core
        )

    each(1, chips, lambda k: swap(k).start())
    swap(0).start()

    def both(k):
        swap(k).wait_recv()
        return x_ref[target(k) * 2 + core].astype(jnp.float32) + near[k].astype(jnp.float32)

    def relay(k):
        pair[k] = both(k).astype(jnp.bfloat16)
        across(k).start()

    each(1, chips, relay)
    total = both(0)

    def add(k, total):
        across(k).wait_recv()
        return total + far[k].astype(jnp.float32)

    for k in range(1, chips):
        total = add(k, total)
    out_ref[...] = total.astype(jnp.bfloat16)
    each(0, chips, lambda k: swap(k).wait_send())
    each(1, chips, lambda k: across(k).wait_send())


def reduce_rows(n, partial):
    dma = pltpu.SemaphoreType.DMA
    half = (n // 2,) + partial.shape[1:]
    return pl.pallas_call(
        functools.partial(reduce_kernel, n),
        out_shape=jax.ShapeDtypeStruct(partial.shape[1:], jnp.bfloat16),
        in_specs=[VMEM],
        out_specs=VMEM,
        scratch_shapes=[pltpu.VMEM(half, jnp.bfloat16)] * 3 + [dma((n // 2,))] * 4,
        compiler_params=pltpu.CompilerParams(
            collective_id=3, has_side_effects=True, vmem_limit_bytes=LIMIT
        ),
    )(partial)


def per_device(
    prefill_rows,
    decode_rows,
    kv_cache,
    slot_lengths,
    prefill_slot,
    norm_gain,
    query_weight,
    keyval_weight,
    output_weight,
):
    n = lax.axis_size("narrow")
    rank = lax.axis_index("narrow")
    steps = decode_rows.shape[1]
    assert decode_rows.shape[0] == 1 and prefill_rows.shape[0] == 1
    height = steps + 1
    width = prefill_rows.shape[1]
    heads = query_weight.shape[0] // HEAD_DIM
    columns = query_weight.shape[1]
    depth = keyval_weight.shape[0]
    rows = jnp.concatenate([decode_rows[0], prefill_rows], axis=0)
    normed = gather_rows(n, rows, norm_gain[None])
    flat = normed.reshape(n * height, width)
    queries = jnp.dot(flat, query_weight, preferred_element_type=jnp.float32)
    queries = queries.astype(jnp.bfloat16)
    part = lax.dynamic_slice_in_dim(flat, rank * depth, depth, 1)
    partial = jnp.dot(part, keyval_weight, preferred_element_type=jnp.float32)
    whole_heads = columns % HEAD_DIM == 0
    if whole_heads:
        local_heads = columns // HEAD_DIM
        block = (n, height * local_heads, HEAD_DIM)
    else:
        local_heads = heads
        block = (n, height, columns)
    queries, new = exchange_queries(
        n, queries.reshape(block), partial.reshape(n, height, 2 * HEAD_DIM)
    )
    if not whole_heads:
        queries = queries.transpose(1, 0, 2)
    chosen = rank == prefill_slot[0]
    live = jnp.where(chosen, 0, slot_lengths[0])
    info = jnp.stack([live, chosen.astype(jnp.int32), rank.astype(jnp.int32)])
    mixed = attend(
        steps,
        height,
        local_heads,
        info,
        queries.reshape(height * heads, HEAD_DIM),
        kv_cache[0],
        new.reshape(n * height, 2 * HEAD_DIM),
    )
    if not whole_heads:
        mixed = mixed.reshape(height, n, columns).transpose(1, 0, 2)
    mixed = exchange_mixed(n, mixed.reshape(block))
    partial = jnp.dot(
        mixed.reshape(n * height, columns), output_weight, preferred_element_type=jnp.float32
    )
    out = reduce_rows(n, partial.astype(jnp.bfloat16).reshape(n, height, width))
    return (out[steps:], out[None, :steps])


def solution(mesh):
    in_specs = (
        P(("group", "narrow"), None),
        P(("group", "narrow"), None, None),
        P(("group", "narrow"), None, None),
        P(("group", "narrow")),
        P("group"),
        P(),
        P(None, "narrow"),
        P("narrow", None),
        P("narrow", None),
    )
    out_specs = (P(("group", "narrow"), None), P(("group", "narrow"), None, None))
    return jax.shard_map(
        per_device, mesh=mesh, in_specs=in_specs, out_specs=out_specs, check_vma=False
    )
```

```python
import functools

import jax
import jax.numpy as jnp
from jax import lax
from jax.experimental import pallas as pl
from jax.experimental.pallas import tpu as pltpu
from jax.sharding import PartitionSpec as P

HEAD_DIM = 128
EPSILON = 1e-05
MESH = pl.DeviceIdType.MESH
VMEM = pl.BlockSpec(memory_space=pltpu.VMEM)
SMEM = pl.BlockSpec(memory_space=pltpu.SMEM)
LIMIT = 40 * 1024 * 1024


def greet(n, me):
    barrier = pltpu.get_barrier_semaphore()

    def hello(k, carry):
        peer = lax.rem(me + k, n)
        pl.semaphore_signal(barrier, inc=1, device_id={"narrow": peer}, device_id_type=MESH)
        return carry

    lax.fori_loop(1, n, hello, 0)
    return barrier


def remote(src, dst, send, recv, peer):
    return pltpu.make_async_remote_copy(
        src_ref=src,
        dst_ref=dst,
        send_sem=send,
        recv_sem=recv,
        device_id={"narrow": peer},
        device_id_type=MESH,
    )


def each(start, stop, body):
    def step(k, carry):
        body(k)
        return carry

    lax.fori_loop(start, stop, step, 0)


def gather_kernel(n, x_ref, gain_ref, out_ref, own, send, recv, fsend, frecv, local):
    me = lax.axis_index("narrow")
    core = lax.rem(me, 2)
    chip = me // 2
    chips = n // 2
    sibling = me + 1 - 2 * core
    barrier = greet(n, me)
    values = x_ref[...].astype(jnp.float32)
    center = values - jnp.mean(values, axis=-1, keepdims=True)
    spread = jnp.mean(center * center, axis=-1, keepdims=True)
    own[...] = (center * lax.rsqrt(spread + EPSILON) * gain_ref[...]).astype(jnp.bfloat16)
    pl.semaphore_wait(barrier, n - 1)

    def across(k):
        to = lax.rem(chip + k, chips) * 2 + core
        return remote(own, out_ref.at[me], send.at[k], recv.at[k], to)

    def arrived(k):
        return lax.rem(chip - k + chips, chips) * 2 + core

    def forward(k):
        src = arrived(k)
        return remote(out_ref.at[src], out_ref.at[src], fsend.at[k], frecv.at[k], sibling)

    each(1, chips, lambda k: across(k).start())
    first = remote(own, out_ref.at[me], fsend.at[0], frecv.at[0], sibling)
    first.start()
    keep = pltpu.make_async_copy(own, out_ref.at[me], local)
    keep.start()

    def relay(k):
        src = arrived(k)
        remote(own, out_ref.at[src], send.at[k], recv.at[k], sibling).wait_recv()
        forward(k).start()

    each(1, chips, relay)
    keep.wait()

    def finish(k):
        src = lax.rem(chip - k + chips, chips) * 2 + 1 - core
        remote(own, out_ref.at[src], fsend.at[k], frecv.at[k], sibling).wait_recv()

    each(0, chips, finish)
    first.wait_send()
    each(1, chips, lambda k: across(k).wait_send())
    each(1, chips, lambda k: forward(k).wait_send())


def gather_rows(n, rows, gain):
    height, width = rows.shape
    dma = pltpu.SemaphoreType.DMA
    return pl.pallas_call(
        functools.partial(gather_kernel, n),
        out_shape=jax.ShapeDtypeStruct((n, height, width), jnp.bfloat16),
        in_specs=[VMEM, VMEM],
        out_specs=VMEM,
        scratch_shapes=[
            pltpu.VMEM((height, width), jnp.bfloat16),
            dma((n // 2,)),
            dma((n // 2,)),
            dma((n // 2,)),
            dma((n // 2,)),
            dma,
        ],
        compiler_params=pltpu.CompilerParams(
            collective_id=0, has_side_effects=True, vmem_limit_bytes=LIMIT
        ),
    )(rows, gain)


def spread_out(n, me, src, dst, send, recv, local):
    def copy(k):
        peer = lax.rem(me + k, n)
        return remote(src.at[peer], dst.at[me], send.at[k], recv.at[k], peer)

    each(1, n, lambda k: copy(k).start())
    keep = pltpu.make_async_copy(src.at[me], dst.at[me], local)
    keep.start()

    def finish():
        keep.wait()

        def take(k):
            peer = lax.rem(me - k + n, n)
            remote(src.at[peer], dst.at[peer], send.at[k], recv.at[k], peer).wait_recv()

        each(1, n, take)
        each(1, n, lambda k: copy(k).wait_send())

    return finish


def query_kernel(
    n, q_ref, kv_ref, qout_ref, kvout_ref, parts, own, qs, qr, ks, kr, bs, br, local
):
    me = lax.axis_index("narrow")
    barrier = greet(n, me)
    pl.semaphore_wait(barrier, n - 1)
    finish_kv = spread_out(n, me, kv_ref, parts, ks, kr, local.at[0])
    finish_q = spread_out(n, me, q_ref, qout_ref, qs, qr, local.at[1])
    finish_kv()
    own[...] = jnp.sum(parts[...], axis=0).astype(jnp.bfloat16)

    def copy(k):
        peer = lax.rem(me + k, n)
        return remote(own, kvout_ref.at[me], bs.at[k], br.at[k], peer)

    each(1, n, lambda k: copy(k).start())
    keep = pltpu.make_async_copy(own, kvout_ref.at[me], local.at[2])
    keep.start()
    finish_q()
    keep.wait()

    def take(k):
        peer = lax.rem(me - k + n, n)
        remote(own, kvout_ref.at[peer], bs.at[k], br.at[k], peer).wait_recv()

    each(1, n, take)
    each(1, n, lambda k: copy(k).wait_send())


def exchange_queries(n, queries, partial):
    dma = pltpu.SemaphoreType.DMA
    return pl.pallas_call(
        functools.partial(query_kernel, n),
        out_shape=(
            jax.ShapeDtypeStruct(queries.shape, jnp.bfloat16),
            jax.ShapeDtypeStruct(partial.shape, jnp.bfloat16),
        ),
        in_specs=[VMEM, VMEM],
        out_specs=(VMEM, VMEM),
        scratch_shapes=[
            pltpu.VMEM(partial.shape, jnp.float32),
            pltpu.VMEM(partial.shape[1:], jnp.bfloat16),
        ]
        + [dma((n,))] * 6
        + [dma((3,))],
        compiler_params=pltpu.CompilerParams(
            collective_id=1, has_side_effects=True, vmem_limit_bytes=LIMIT
        ),
    )(queries, partial)


def attend_kernel(steps, height, local_heads, info_ref, q_ref, cache_ref, new_ref, out_ref):
    live, chosen, me = info_ref[0], info_ref[1], info_ref[2]
    queries = q_ref[...]
    count = queries.shape[0]
    scale = HEAD_DIM ** (-0.5)

    def scores_of(ref):
        return scale * lax.dot_general(
            queries,
            ref[:, :HEAD_DIM],
            (((1,), (1,)), ((), ())),
            preferred_element_type=jnp.float32,
        )

    row = lax.broadcasted_iota(jnp.int32, (count, 1), 0)
    token = lax.rem(row, height * local_heads) // local_heads
    limit = jnp.where(token < steps, live, 0)
    depth = cache_ref.shape[0]
    position = lax.broadcasted_iota(jnp.int32, (count, depth), 1)
    old = jnp.where(position < limit, scores_of(cache_ref), -1e30)
    fresh_count = new_ref.shape[0]
    column = lax.broadcasted_iota(jnp.int32, (count, fresh_count), 1)
    owner = column // height
    kind = lax.rem(column, height)
    reach = jnp.where(token < steps, jnp.where(chosen > 0, fresh_count, -1), me)
    from_prefill = (kind == steps) & (owner <= reach)
    from_steps = (kind < steps) & (kind <= token) & (token < steps) & (owner == me)
    new = jnp.where(from_prefill | from_steps, scores_of(new_ref), -1e30)
    highest = jnp.maximum(
        jnp.max(old, axis=-1, keepdims=True), jnp.max(new, axis=-1, keepdims=True)
    )
    old = jnp.exp(old - highest)
    new = jnp.exp(new - highest)
    total = jnp.sum(old, axis=-1, keepdims=True) + jnp.sum(new, axis=-1, keepdims=True)
    mixed = jnp.dot(
        old.astype(jnp.bfloat16), cache_ref[:, HEAD_DIM:], preferred_element_type=jnp.float32
    )
    mixed = mixed + jnp.dot(
        new.astype(jnp.bfloat16), new_ref[:, HEAD_DIM:], preferred_element_type=jnp.float32
    )
    out_ref[...] = (mixed / total).astype(jnp.bfloat16)


def attend(steps, height, local_heads, info, queries, cache, new):
    return pl.pallas_call(
        functools.partial(attend_kernel, steps, height, local_heads),
        out_shape=jax.ShapeDtypeStruct(queries.shape, jnp.bfloat16),
        in_specs=[SMEM, VMEM, VMEM, VMEM],
        out_specs=VMEM,
        compiler_params=pltpu.CompilerParams(vmem_limit_bytes=LIMIT),
    )(info, queries, cache, new)


def mixed_kernel(n, x_ref, out_ref, send, recv, local):
    me = lax.axis_index("narrow")
    barrier = greet(n, me)
    pl.semaphore_wait(barrier, n - 1)
    spread_out(n, me, x_ref, out_ref, send, recv, local)()


def exchange_mixed(n, mixed):
    dma = pltpu.SemaphoreType.DMA
    return pl.pallas_call(
        functools.partial(mixed_kernel, n),
        out_shape=jax.ShapeDtypeStruct(mixed.shape, mixed.dtype),
        in_specs=[VMEM],
        out_specs=VMEM,
        scratch_shapes=[dma((n,)), dma((n,)), dma],
        compiler_params=pltpu.CompilerParams(
            collective_id=2, has_side_effects=True, vmem_limit_bytes=LIMIT
        ),
    )(mixed)


def reduce_kernel(n, x_ref, out_ref, near, pair, far, psend, precv, send, recv):
    me = lax.axis_index("narrow")
    core = lax.rem(me, 2)
    chip = me // 2
    chips = n // 2
    sibling = me + 1 - 2 * core
    barrier = greet(n, me)
    pl.semaphore_wait(barrier, n - 1)

    def target(k):
        return lax.rem(chip + k, chips)

    def swap(k):
        return remote(
            x_ref.at[target(k) * 2 + 1 - core],
            near.at[k],
            psend.at[k],
            precv.at[k],
            sibling,
        )

    def across(k):
        return remote(
            pair.at[k], far.at[k], send.at[k], recv.at[k], target(k) * 2 + core
        )

    each(1, chips, lambda k: swap(k).start())
    swap(0).start()

    def both(k):
        swap(k).wait_recv()
        return x_ref[target(k) * 2 + core].astype(jnp.float32) + near[k].astype(jnp.float32)

    def relay(k):
        pair[k] = both(k).astype(jnp.bfloat16)
        across(k).start()

    each(1, chips, relay)
    total = both(0)

    def add(k, total):
        across(k).wait_recv()
        return total + far[k].astype(jnp.float32)

    for k in range(1, chips):
        total = add(k, total)
    out_ref[...] = total.astype(jnp.bfloat16)
    each(0, chips, lambda k: swap(k).wait_send())
    each(1, chips, lambda k: across(k).wait_send())


def reduce_rows(n, partial):
    dma = pltpu.SemaphoreType.DMA
    half = (n // 2,) + partial.shape[1:]
    return pl.pallas_call(
        functools.partial(reduce_kernel, n),
        out_shape=jax.ShapeDtypeStruct(partial.shape[1:], jnp.bfloat16),
        in_specs=[VMEM],
        out_specs=VMEM,
        scratch_shapes=[pltpu.VMEM(half, jnp.bfloat16)] * 3 + [dma((n // 2,))] * 4,
        compiler_params=pltpu.CompilerParams(
            collective_id=3, has_side_effects=True, vmem_limit_bytes=LIMIT
        ),
    )(partial)


def fused_kernel(
    n,
    steps,
    local_heads,
    length_ref,
    slot_ref,
    prefill_ref,
    decode_ref,
    gain_ref,
    cache_hbm,
    wq_hbm,
    wkv_hbm,
    wo_hbm,
    pre_out,
    dec_out,
    cache,
    wq,
    wkv,
    wo,
    own,
    rows,
    q_from,
    q_to,
    kv_from,
    kv_to,
    kv_own,
    new_ref,
    mix_from,
    mix_to,
    part,
    near,
    pair,
    far,
    load,
    gs,
    gr,
    fs,
    fr,
    qs,
    qr,
    ks,
    kr,
    bs,
    br,
    ms,
    mr,
    ps,
    pr,
    ss,
    sr,
):
    me = lax.axis_index("narrow")
    core = lax.rem(me, 2)
    chip = me // 2
    chips = n // 2
    sibling = me + 1 - 2 * core
    chunks, height, wide = own.shape
    depth = wkv.shape[0]
    columns = wq.shape[1]
    barrier = greet(n, me)
    loads = [
        pltpu.make_async_copy(src, dst, load.at[i])
        for i, (src, dst) in enumerate(
            ((wq_hbm, wq), (wkv_hbm, wkv), (cache_hbm, cache), (wo_hbm, wo))
        )
    ]
    for copy in loads:
        copy.start()
    values = jnp.concatenate(
        [decode_ref[...].astype(jnp.float32), prefill_ref[...].astype(jnp.float32)], axis=0
    )
    center = values - jnp.mean(values, axis=-1, keepdims=True)
    spread = jnp.mean(center * center, axis=-1, keepdims=True)
    normed = (center * lax.rsqrt(spread + EPSILON) * gain_ref[...]).astype(jnp.bfloat16)
    for c in range(chunks):
        own[c] = normed[:, c * wide : (c + 1) * wide]
        rows[c, me] = normed[:, c * wide : (c + 1) * wide]
    pl.semaphore_wait(barrier, n - 1)

    def target(k):
        return lax.rem(chip + k, chips)

    def source(k):
        return lax.rem(chip - k + chips, chips)

    def across(c, k):
        to = target(k) * 2 + core
        return remote(own.at[c], rows.at[c, me], gs.at[c, k], gr.at[c, k], to)

    def first(c):
        return remote(own.at[c], rows.at[c, me], fs.at[c, 0], fr.at[c, 0], sibling)

    def forward(c, k):
        block = rows.at[c, source(k) * 2 + core]
        return remote(block, block, fs.at[c, k], fr.at[c, k], sibling)

    for c in range(chunks):
        each(1, chips, lambda k: across(c, k).start())
        first(c).start()

    def relay(c):
        def step(k):
            block = rows.at[c, source(k) * 2 + core]
            remote(own.at[c], block, gs.at[c, k], gr.at[c, k], sibling).wait_recv()
            forward(c, k).start()

        each(1, chips, step)

    def gathered(c):
        def step(k):
            block = rows.at[c, source(k) * 2 + 1 - core]
            remote(own.at[c], block, fs.at[c, k], fr.at[c, k], sibling).wait_recv()

        each(0, chips, step)

    def project(c):
        return jnp.dot(
            rows[c].reshape(n * height, wide),
            wq[c * wide : (c + 1) * wide, :],
            preferred_element_type=jnp.float32,
        )

    def start_all(src, dst, send, recv):
        def copy(k):
            peer = lax.rem(me + k, n)
            block = src.at[peer] if len(src.shape) == len(dst.shape) else src
            return remote(block, dst.at[me], send.at[k], recv.at[k], peer)

        each(1, n, lambda k: copy(k).start())

        def arrive():
            def take(k):
                peer = lax.rem(me - k + n, n)
                block = src.at[peer] if len(src.shape) == len(dst.shape) else src
                remote(block, dst.at[peer], send.at[k], recv.at[k], peer).wait_recv()

            each(1, n, take)

        return arrive, lambda: each(1, n, lambda k: copy(k).wait_send())

    relay(0)
    queries = jnp.zeros((n * height, columns), jnp.float32)
    for c in range(chunks):
        if c + 1 < chunks:
            relay(c + 1)
        gathered(c)
        if c == 0:
            loads[0].wait()
        if c + 1 == chunks:
            loads[1].wait()
            share = n // chunks
            start = pl.multiple_of(lax.rem(me, share) * depth, 128)
            piece = rows[me // share, :, :, pl.ds(start, depth)].reshape(n * height, depth)
            partial = jnp.dot(piece, wkv[...], preferred_element_type=jnp.float32)
            kv_from[...] = partial.reshape(n, height, 2 * HEAD_DIM)
            kv_to[me] = kv_from[me]
            kv_arrive, kv_sent = start_all(kv_from, kv_to, ks, kr)
        queries = queries + project(c)
    q_from[...] = queries.reshape(n, height * local_heads, HEAD_DIM).astype(jnp.bfloat16)
    q_to[me] = q_from[me]
    q_arrive, q_sent = start_all(q_from, q_to, qs, qr)
    kv_arrive()
    fresh = jnp.sum(kv_to[...], axis=0).astype(jnp.bfloat16)
    kv_own[...] = fresh
    new_ref[me] = fresh
    new_arrive, new_sent = start_all(kv_own, new_ref, bs, br)
    q_arrive()

    block_rows = height * local_heads
    count = n * block_rows
    own_queries = q_to[...].reshape(count, HEAD_DIM)
    scale = HEAD_DIM ** (-0.5)

    def scores_of(keys):
        return scale * lax.dot_general(
            own_queries, keys, (((1,), (1,)), ((), ())), preferred_element_type=jnp.float32
        )

    chosen = slot_ref[0] == me
    live = jnp.where(chosen, 0, length_ref[0])
    token = lax.rem(lax.broadcasted_iota(jnp.int32, (count, 1), 0), block_rows) // local_heads
    limit = jnp.where(token < steps, live, 0)
    loads[2].wait()
    position = lax.broadcasted_iota(jnp.int32, (count, cache.shape[0]), 1)
    old = jnp.where(position < limit, scores_of(cache[:, :HEAD_DIM]), -1e30)
    highest = jnp.max(old, axis=-1, keepdims=True)
    new_arrive()
    keyvals = new_ref[...].reshape(n * height, 2 * HEAD_DIM)
    column = lax.broadcasted_iota(jnp.int32, (count, n * height), 1)
    owner = column // height
    kind = lax.rem(column, height)
    reach = jnp.where(token < steps, jnp.where(chosen, n, -1), me)
    from_prefill = (kind == steps) & (owner <= reach)
    from_steps = (kind < steps) & (kind <= token) & (token < steps) & (owner == me)
    new = jnp.where(from_prefill | from_steps, scores_of(keyvals[:, :HEAD_DIM]), -1e30)
    highest = jnp.maximum(highest, jnp.max(new, axis=-1, keepdims=True))
    old = jnp.exp(old - highest)
    new = jnp.exp(new - highest)
    total = jnp.sum(old, axis=-1, keepdims=True) + jnp.sum(new, axis=-1, keepdims=True)
    mixed = jnp.dot(
        old.astype(jnp.bfloat16), cache[:, HEAD_DIM:], preferred_element_type=jnp.float32
    )
    mixed = mixed + jnp.dot(
        new.astype(jnp.bfloat16), keyvals[:, HEAD_DIM:], preferred_element_type=jnp.float32
    )
    mix_from[...] = (mixed / total).reshape(n, block_rows, HEAD_DIM).astype(jnp.bfloat16)
    mix_to[me] = mix_from[me]
    mix_arrive, mix_sent = start_all(mix_from, mix_to, ms, mr)
    loads[3].wait()
    mix_arrive()
    flat = mix_to[...].astype(jnp.float32).reshape(n * height, columns).astype(jnp.bfloat16)

    def swap(e):
        return remote(part.at[e, 1 - core], near.at[e], ps.at[e], pr.at[e], sibling)

    def out_across(e, k):
        to = target(k)
        return remote(
            pair.at[e, to], far.at[e, chip], ss.at[e, k], sr.at[e, k], to * 2 + core
        )

    def fold(e):
        swap(e).wait_recv()
        both = part[e, core].astype(jnp.float32) + near[e].astype(jnp.float32)
        pair[e] = both.astype(jnp.bfloat16)
        each(1, chips, lambda k: out_across(e, k).start())
        far[e, chip] = pair[e, chip]

    for e in range(chunks):
        product = jnp.dot(
            flat, wo[:, e * wide : (e + 1) * wide], preferred_element_type=jnp.float32
        )
        product = product.reshape(chips, 2, height, wide).astype(jnp.bfloat16)
        part[e, 0] = product[:, 0]
        part[e, 1] = product[:, 1]
        swap(e).start()
        if e > 0:
            fold(e - 1)
    fold(chunks - 1)
    for e in range(chunks):

        def take(k):
            remote(
                pair.at[e, 0], far.at[e, source(k)], ss.at[e, k], sr.at[e, k], sibling
            ).wait_recv()

        each(1, chips, take)
        result = jnp.sum(far[e].astype(jnp.float32), axis=0).astype(jnp.bfloat16)
        dec_out[:, e * wide : (e + 1) * wide] = result[:steps]
        pre_out[:, e * wide : (e + 1) * wide] = result[steps:]
    for c in range(chunks):
        each(1, chips, lambda k: across(c, k).wait_send())
        first(c).wait_send()
        each(1, chips, lambda k: forward(c, k).wait_send())
        swap(c).wait_send()
        each(1, chips, lambda k: out_across(c, k).wait_send())
    kv_sent()
    q_sent()
    new_sent()
    mix_sent()


def fused(n, prefill, decode, cache, length, slot, gain, wq, wkv, wo):
    dma = pltpu.SemaphoreType.DMA
    steps, width = decode.shape
    height = steps + 1
    columns = wq.shape[1]
    local_heads = columns // HEAD_DIM
    chunks = 4
    wide = width // chunks
    chips = n // 2
    heads_block = (n, height * local_heads, HEAD_DIM)
    new_block = (n, height, 2 * HEAD_DIM)
    half = (chunks, chips, height, wide)
    narrow = jnp.bfloat16
    hbm = pl.BlockSpec(memory_space=pltpu.HBM)
    return pl.pallas_call(
        functools.partial(fused_kernel, n, steps, local_heads),
        out_shape=(
            jax.ShapeDtypeStruct(prefill.shape, narrow),
            jax.ShapeDtypeStruct(decode.shape, narrow),
        ),
        in_specs=[SMEM, SMEM, VMEM, VMEM, VMEM, hbm, hbm, hbm, hbm],
        out_specs=(VMEM, VMEM),
        scratch_shapes=[
            pltpu.VMEM(cache.shape, narrow),
            pltpu.VMEM(wq.shape, narrow),
            pltpu.VMEM(wkv.shape, narrow),
            pltpu.VMEM(wo.shape, narrow),
            pltpu.VMEM((chunks, height, wide), narrow),
            pltpu.VMEM((chunks, n, height, wide), narrow),
            pltpu.VMEM(heads_block, narrow),
            pltpu.VMEM(heads_block, narrow),
            pltpu.VMEM(new_block, jnp.float32),
            pltpu.VMEM(new_block, jnp.float32),
            pltpu.VMEM(new_block[1:], narrow),
            pltpu.VMEM(new_block, narrow),
            pltpu.VMEM(heads_block, narrow),
            pltpu.VMEM(heads_block, narrow),
            pltpu.VMEM((chunks, 2, chips, height, wide), narrow),
            pltpu.VMEM(half, narrow),
            pltpu.VMEM(half, narrow),
            pltpu.VMEM(half, narrow),
            dma((4,)),
        ]
        + [dma((chunks, chips))] * 4
        + [dma((n,))] * 8
        + [dma((chunks,))] * 2
        + [dma((chunks, chips))] * 2,
        compiler_params=pltpu.CompilerParams(
            collective_id=4, has_side_effects=True, vmem_limit_bytes=48 * 1024 * 1024
        ),
    )(length, slot, prefill, decode, gain, cache, wq, wkv, wo)


def per_device(
    prefill_rows,
    decode_rows,
    kv_cache,
    slot_lengths,
    prefill_slot,
    norm_gain,
    query_weight,
    keyval_weight,
    output_weight,
):
    n = lax.axis_size("narrow")
    rank = lax.axis_index("narrow")
    steps = decode_rows.shape[1]
    assert decode_rows.shape[0] == 1 and prefill_rows.shape[0] == 1
    height = steps + 1
    width = prefill_rows.shape[1]
    heads = query_weight.shape[0] // HEAD_DIM
    columns = query_weight.shape[1]
    depth = keyval_weight.shape[0]
    if columns % HEAD_DIM == 0 and n % 4 == 0 and depth % HEAD_DIM == 0:
        prefill_out, decode_out = fused(
            n,
            prefill_rows,
            decode_rows[0],
            kv_cache[0],
            slot_lengths,
            prefill_slot,
            norm_gain[None],
            query_weight,
            keyval_weight,
            output_weight,
        )
        return (prefill_out, decode_out[None])
    rows = jnp.concatenate([decode_rows[0], prefill_rows], axis=0)
    normed = gather_rows(n, rows, norm_gain[None])
    flat = normed.reshape(n * height, width)
    queries = jnp.dot(flat, query_weight, preferred_element_type=jnp.float32)
    queries = queries.astype(jnp.bfloat16)
    part = lax.dynamic_slice_in_dim(flat, rank * depth, depth, 1)
    partial = jnp.dot(part, keyval_weight, preferred_element_type=jnp.float32)
    whole_heads = columns % HEAD_DIM == 0
    if whole_heads:
        local_heads = columns // HEAD_DIM
        block = (n, height * local_heads, HEAD_DIM)
    else:
        local_heads = heads
        block = (n, height, columns)
    queries, new = exchange_queries(
        n, queries.reshape(block), partial.reshape(n, height, 2 * HEAD_DIM)
    )
    if not whole_heads:
        queries = queries.transpose(1, 0, 2)
    chosen = rank == prefill_slot[0]
    live = jnp.where(chosen, 0, slot_lengths[0])
    info = jnp.stack([live, chosen.astype(jnp.int32), rank.astype(jnp.int32)])
    mixed = attend(
        steps,
        height,
        local_heads,
        info,
        queries.reshape(height * heads, HEAD_DIM),
        kv_cache[0],
        new.reshape(n * height, 2 * HEAD_DIM),
    )
    if not whole_heads:
        mixed = mixed.reshape(height, n, columns).transpose(1, 0, 2)
    mixed = exchange_mixed(n, mixed.reshape(block))
    partial = jnp.dot(
        mixed.reshape(n * height, columns), output_weight, preferred_element_type=jnp.float32
    )
    out = reduce_rows(n, partial.astype(jnp.bfloat16).reshape(n, height, width))
    return (out[steps:], out[None, :steps])


def solution(mesh):
    in_specs = (
        P(("group", "narrow"), None),
        P(("group", "narrow"), None, None),
        P(("group", "narrow"), None, None),
        P(("group", "narrow")),
        P("group"),
        P(),
        P(None, "narrow"),
        P("narrow", None),
        P("narrow", None),
    )
    out_specs = (P(("group", "narrow"), None), P(("group", "narrow"), None, None))
    return jax.shard_map(
        per_device, mesh=mesh, in_specs=in_specs, out_specs=out_specs, check_vma=False
    )
```

```python
import functools

import jax
import jax.numpy as jnp
from jax import lax
from jax.experimental import pallas as pl
from jax.experimental.pallas import tpu as pltpu
from jax.sharding import PartitionSpec as P

HEAD_DIM = 128
EPSILON = 1e-05
MESH = pl.DeviceIdType.MESH
VMEM = pl.BlockSpec(memory_space=pltpu.VMEM)
SMEM = pl.BlockSpec(memory_space=pltpu.SMEM)
LIMIT = 40 * 1024 * 1024


def greet(n, me):
    barrier = pltpu.get_barrier_semaphore()

    def hello(k, carry):
        peer = lax.rem(me + k, n)
        pl.semaphore_signal(barrier, inc=1, device_id={"narrow": peer}, device_id_type=MESH)
        return carry

    lax.fori_loop(1, n, hello, 0)
    return barrier


def remote(src, dst, send, recv, peer):
    return pltpu.make_async_remote_copy(
        src_ref=src,
        dst_ref=dst,
        send_sem=send,
        recv_sem=recv,
        device_id={"narrow": peer},
        device_id_type=MESH,
    )


def each(start, stop, body):
    def step(k, carry):
        body(k)
        return carry

    lax.fori_loop(start, stop, step, 0)


def gather_kernel(n, x_ref, gain_ref, out_ref, own, send, recv, fsend, frecv, local):
    me = lax.axis_index("narrow")
    core = lax.rem(me, 2)
    chip = me // 2
    chips = n // 2
    sibling = me + 1 - 2 * core
    barrier = greet(n, me)
    values = x_ref[...].astype(jnp.float32)
    center = values - jnp.mean(values, axis=-1, keepdims=True)
    spread = jnp.mean(center * center, axis=-1, keepdims=True)
    own[...] = (center * lax.rsqrt(spread + EPSILON) * gain_ref[...]).astype(jnp.bfloat16)
    pl.semaphore_wait(barrier, n - 1)

    def across(k):
        to = lax.rem(chip + k, chips) * 2 + core
        return remote(own, out_ref.at[me], send.at[k], recv.at[k], to)

    def arrived(k):
        return lax.rem(chip - k + chips, chips) * 2 + core

    def forward(k):
        src = arrived(k)
        return remote(out_ref.at[src], out_ref.at[src], fsend.at[k], frecv.at[k], sibling)

    each(1, chips, lambda k: across(k).start())
    first = remote(own, out_ref.at[me], fsend.at[0], frecv.at[0], sibling)
    first.start()
    keep = pltpu.make_async_copy(own, out_ref.at[me], local)
    keep.start()

    def relay(k):
        src = arrived(k)
        remote(own, out_ref.at[src], send.at[k], recv.at[k], sibling).wait_recv()
        forward(k).start()

    each(1, chips, relay)
    keep.wait()

    def finish(k):
        src = lax.rem(chip - k + chips, chips) * 2 + 1 - core
        remote(own, out_ref.at[src], fsend.at[k], frecv.at[k], sibling).wait_recv()

    each(0, chips, finish)
    first.wait_send()
    each(1, chips, lambda k: across(k).wait_send())
    each(1, chips, lambda k: forward(k).wait_send())


def gather_rows(n, rows, gain):
    height, width = rows.shape
    dma = pltpu.SemaphoreType.DMA
    return pl.pallas_call(
        functools.partial(gather_kernel, n),
        out_shape=jax.ShapeDtypeStruct((n, height, width), jnp.bfloat16),
        in_specs=[VMEM, VMEM],
        out_specs=VMEM,
        scratch_shapes=[
            pltpu.VMEM((height, width), jnp.bfloat16),
            dma((n // 2,)),
            dma((n // 2,)),
            dma((n // 2,)),
            dma((n // 2,)),
            dma,
        ],
        compiler_params=pltpu.CompilerParams(
            collective_id=0, has_side_effects=True, vmem_limit_bytes=LIMIT
        ),
    )(rows, gain)


def spread_out(n, me, src, dst, send, recv, local):
    def copy(k):
        peer = lax.rem(me + k, n)
        return remote(src.at[peer], dst.at[me], send.at[k], recv.at[k], peer)

    each(1, n, lambda k: copy(k).start())
    keep = pltpu.make_async_copy(src.at[me], dst.at[me], local)
    keep.start()

    def finish():
        keep.wait()

        def take(k):
            peer = lax.rem(me - k + n, n)
            remote(src.at[peer], dst.at[peer], send.at[k], recv.at[k], peer).wait_recv()

        each(1, n, take)
        each(1, n, lambda k: copy(k).wait_send())

    return finish


def query_kernel(
    n, q_ref, kv_ref, qout_ref, kvout_ref, parts, own, qs, qr, ks, kr, bs, br, local
):
    me = lax.axis_index("narrow")
    barrier = greet(n, me)
    pl.semaphore_wait(barrier, n - 1)
    finish_kv = spread_out(n, me, kv_ref, parts, ks, kr, local.at[0])
    finish_q = spread_out(n, me, q_ref, qout_ref, qs, qr, local.at[1])
    finish_kv()
    own[...] = jnp.sum(parts[...], axis=0).astype(jnp.bfloat16)

    def copy(k):
        peer = lax.rem(me + k, n)
        return remote(own, kvout_ref.at[me], bs.at[k], br.at[k], peer)

    each(1, n, lambda k: copy(k).start())
    keep = pltpu.make_async_copy(own, kvout_ref.at[me], local.at[2])
    keep.start()
    finish_q()
    keep.wait()

    def take(k):
        peer = lax.rem(me - k + n, n)
        remote(own, kvout_ref.at[peer], bs.at[k], br.at[k], peer).wait_recv()

    each(1, n, take)
    each(1, n, lambda k: copy(k).wait_send())


def exchange_queries(n, queries, partial):
    dma = pltpu.SemaphoreType.DMA
    return pl.pallas_call(
        functools.partial(query_kernel, n),
        out_shape=(
            jax.ShapeDtypeStruct(queries.shape, jnp.bfloat16),
            jax.ShapeDtypeStruct(partial.shape, jnp.bfloat16),
        ),
        in_specs=[VMEM, VMEM],
        out_specs=(VMEM, VMEM),
        scratch_shapes=[
            pltpu.VMEM(partial.shape, jnp.float32),
            pltpu.VMEM(partial.shape[1:], jnp.bfloat16),
        ]
        + [dma((n,))] * 6
        + [dma((3,))],
        compiler_params=pltpu.CompilerParams(
            collective_id=1, has_side_effects=True, vmem_limit_bytes=LIMIT
        ),
    )(queries, partial)


def attend_kernel(steps, height, local_heads, info_ref, q_ref, cache_ref, new_ref, out_ref):
    live, chosen, me = info_ref[0], info_ref[1], info_ref[2]
    queries = q_ref[...]
    count = queries.shape[0]
    scale = HEAD_DIM ** (-0.5)

    def scores_of(ref):
        return scale * lax.dot_general(
            queries,
            ref[:, :HEAD_DIM],
            (((1,), (1,)), ((), ())),
            preferred_element_type=jnp.float32,
        )

    row = lax.broadcasted_iota(jnp.int32, (count, 1), 0)
    token = lax.rem(row, height * local_heads) // local_heads
    limit = jnp.where(token < steps, live, 0)
    depth = cache_ref.shape[0]
    position = lax.broadcasted_iota(jnp.int32, (count, depth), 1)
    old = jnp.where(position < limit, scores_of(cache_ref), -1e30)
    fresh_count = new_ref.shape[0]
    column = lax.broadcasted_iota(jnp.int32, (count, fresh_count), 1)
    owner = column // height
    kind = lax.rem(column, height)
    reach = jnp.where(token < steps, jnp.where(chosen > 0, fresh_count, -1), me)
    from_prefill = (kind == steps) & (owner <= reach)
    from_steps = (kind < steps) & (kind <= token) & (token < steps) & (owner == me)
    new = jnp.where(from_prefill | from_steps, scores_of(new_ref), -1e30)
    highest = jnp.maximum(
        jnp.max(old, axis=-1, keepdims=True), jnp.max(new, axis=-1, keepdims=True)
    )
    old = jnp.exp(old - highest)
    new = jnp.exp(new - highest)
    total = jnp.sum(old, axis=-1, keepdims=True) + jnp.sum(new, axis=-1, keepdims=True)
    mixed = jnp.dot(
        old.astype(jnp.bfloat16), cache_ref[:, HEAD_DIM:], preferred_element_type=jnp.float32
    )
    mixed = mixed + jnp.dot(
        new.astype(jnp.bfloat16), new_ref[:, HEAD_DIM:], preferred_element_type=jnp.float32
    )
    out_ref[...] = (mixed / total).astype(jnp.bfloat16)


def attend(steps, height, local_heads, info, queries, cache, new):
    return pl.pallas_call(
        functools.partial(attend_kernel, steps, height, local_heads),
        out_shape=jax.ShapeDtypeStruct(queries.shape, jnp.bfloat16),
        in_specs=[SMEM, VMEM, VMEM, VMEM],
        out_specs=VMEM,
        compiler_params=pltpu.CompilerParams(vmem_limit_bytes=LIMIT),
    )(info, queries, cache, new)


def mixed_kernel(n, x_ref, out_ref, send, recv, local):
    me = lax.axis_index("narrow")
    barrier = greet(n, me)
    pl.semaphore_wait(barrier, n - 1)
    spread_out(n, me, x_ref, out_ref, send, recv, local)()


def exchange_mixed(n, mixed):
    dma = pltpu.SemaphoreType.DMA
    return pl.pallas_call(
        functools.partial(mixed_kernel, n),
        out_shape=jax.ShapeDtypeStruct(mixed.shape, mixed.dtype),
        in_specs=[VMEM],
        out_specs=VMEM,
        scratch_shapes=[dma((n,)), dma((n,)), dma],
        compiler_params=pltpu.CompilerParams(
            collective_id=2, has_side_effects=True, vmem_limit_bytes=LIMIT
        ),
    )(mixed)


def reduce_kernel(n, x_ref, out_ref, near, pair, far, psend, precv, send, recv):
    me = lax.axis_index("narrow")
    core = lax.rem(me, 2)
    chip = me // 2
    chips = n // 2
    sibling = me + 1 - 2 * core
    barrier = greet(n, me)
    pl.semaphore_wait(barrier, n - 1)

    def target(k):
        return lax.rem(chip + k, chips)

    def swap(k):
        return remote(
            x_ref.at[target(k) * 2 + 1 - core],
            near.at[k],
            psend.at[k],
            precv.at[k],
            sibling,
        )

    def across(k):
        return remote(
            pair.at[k], far.at[k], send.at[k], recv.at[k], target(k) * 2 + core
        )

    each(1, chips, lambda k: swap(k).start())
    swap(0).start()

    def both(k):
        swap(k).wait_recv()
        return x_ref[target(k) * 2 + core].astype(jnp.float32) + near[k].astype(jnp.float32)

    def relay(k):
        pair[k] = both(k).astype(jnp.bfloat16)
        across(k).start()

    each(1, chips, relay)
    total = both(0)

    def add(k, total):
        across(k).wait_recv()
        return total + far[k].astype(jnp.float32)

    for k in range(1, chips):
        total = add(k, total)
    out_ref[...] = total.astype(jnp.bfloat16)
    each(0, chips, lambda k: swap(k).wait_send())
    each(1, chips, lambda k: across(k).wait_send())


def reduce_rows(n, partial):
    dma = pltpu.SemaphoreType.DMA
    half = (n // 2,) + partial.shape[1:]
    return pl.pallas_call(
        functools.partial(reduce_kernel, n),
        out_shape=jax.ShapeDtypeStruct(partial.shape[1:], jnp.bfloat16),
        in_specs=[VMEM],
        out_specs=VMEM,
        scratch_shapes=[pltpu.VMEM(half, jnp.bfloat16)] * 3 + [dma((n // 2,))] * 4,
        compiler_params=pltpu.CompilerParams(
            collective_id=3, has_side_effects=True, vmem_limit_bytes=LIMIT
        ),
    )(partial)


def fused_kernel(
    n,
    steps,
    local_heads,
    length_ref,
    slot_ref,
    prefill_ref,
    decode_ref,
    gain_ref,
    cache_hbm,
    wq_hbm,
    wkv_hbm,
    wo_hbm,
    pre_out,
    dec_out,
    cache,
    wq,
    wkv,
    wo,
    rows,
    q_from,
    q_to,
    kv_from,
    kv_to,
    kv_own,
    new_ref,
    mix_from,
    mix_to,
    part,
    near,
    pair,
    far,
    load,
    gs,
    gr,
    fs,
    fr,
    qs,
    qr,
    ks,
    kr,
    bs,
    br,
    ms,
    mr,
    ps,
    pr,
    ss,
    sr,
):
    me = lax.axis_index("narrow")
    core = lax.rem(me, 2)
    chip = me // 2
    chips = n // 2
    sibling = me + 1 - 2 * core
    chunks, height, wide = rows.shape[0], rows.shape[3], rows.shape[4]
    depth = wkv.shape[0]
    columns = wq.shape[1]
    barrier = greet(n, me)
    loads = [
        pltpu.make_async_copy(src, dst, load.at[i])
        for i, (src, dst) in enumerate(
            ((wq_hbm, wq), (wkv_hbm, wkv), (cache_hbm, cache), (wo_hbm, wo))
        )
    ]
    for copy in loads:
        copy.start()
    values = jnp.concatenate(
        [decode_ref[...].astype(jnp.float32), prefill_ref[...].astype(jnp.float32)], axis=0
    )
    center = values - jnp.mean(values, axis=-1, keepdims=True)
    spread = jnp.mean(center * center, axis=-1, keepdims=True)
    normed = (center * lax.rsqrt(spread + EPSILON) * gain_ref[...]).astype(jnp.bfloat16)
    for c in range(chunks):
        rows[c, core, chip] = normed[:, c * wide : (c + 1) * wide]
    pl.semaphore_wait(barrier, n - 1)
    place = core * chips + chip

    def target(k):
        return lax.rem(chip + k, chips)

    def across(c, k):
        block = rows.at[c, core, chip]
        return remote(block, block, gs.at[c], gr.at[c], target(k) * 2 + core)

    def across_all(c):
        block = rows.at[c, core, pl.ds(0, chips - 1)]
        return remote(block, block, gs.at[c], gr.at[c], sibling)

    def forward(c):
        block = rows.at[c, core]
        return remote(block, block, fs.at[c], fr.at[c], sibling)

    def backward(c):
        block = rows.at[c, 1 - core]
        return remote(block, block, fs.at[c], fr.at[c], sibling)

    for c in range(chunks):
        each(1, chips, lambda k: across(c, k).start())

    def relay(c):
        across_all(c).wait_recv()
        forward(c).start()

    def gathered(c):
        backward(c).wait_recv()

    def project(c):
        return jnp.dot(
            rows[c].reshape(n * height, wide),
            wq[c * wide : (c + 1) * wide, :],
            preferred_element_type=jnp.float32,
        )

    def start_all(src, dst, send, recv):
        def copy(k):
            peer = lax.rem(me + k, n)
            spot = lax.rem(peer, 2) * chips + peer // 2
            block = src.at[spot] if len(src.shape) == len(dst.shape) else src
            return remote(block, dst.at[place], send, recv, peer)

        each(1, n, lambda k: copy(k).start())
        many = dst.at[pl.ds(0, n - 1)]
        every = remote(many, many, send, recv, sibling)
        return every.wait_recv, every.wait_send

    relay(0)
    queries = jnp.zeros((n * height, columns), jnp.float32)
    for c in range(chunks):
        if c + 1 < chunks:
            relay(c + 1)
        gathered(c)
        if c == 0:
            loads[0].wait()
        if c + 1 == chunks:
            loads[1].wait()
            share = n // chunks
            start = pl.multiple_of(lax.rem(me, share) * depth, 128)
            piece = rows[me // share, :, :, :, pl.ds(start, depth)].reshape(n * height, depth)
            partial = jnp.dot(piece, wkv[...], preferred_element_type=jnp.float32)
            kv_from[...] = partial.reshape(n, height, 2 * HEAD_DIM)
            kv_to[place] = kv_from[place]
            kv_arrive, kv_sent = start_all(kv_from, kv_to, ks.at[0], kr.at[0])
        queries = queries + project(c)
    q_from[...] = queries.reshape(n, height * local_heads, HEAD_DIM).astype(jnp.bfloat16)
    q_to[place] = q_from[place]
    q_arrive, q_sent = start_all(q_from, q_to, qs.at[0], qr.at[0])
    kv_arrive()
    fresh = jnp.sum(kv_to[...], axis=0).astype(jnp.bfloat16)
    kv_own[...] = fresh
    new_ref[place] = fresh
    new_arrive, new_sent = start_all(kv_own, new_ref, bs.at[0], br.at[0])
    q_arrive()

    block_rows = height * local_heads
    count = n * block_rows
    own_queries = q_to[...].reshape(count, HEAD_DIM)
    scale = HEAD_DIM ** (-0.5)

    def scores_of(keys):
        return scale * lax.dot_general(
            own_queries, keys, (((1,), (1,)), ((), ())), preferred_element_type=jnp.float32
        )

    chosen = slot_ref[0] == me
    live = jnp.where(chosen, 0, length_ref[0])
    token = lax.rem(lax.broadcasted_iota(jnp.int32, (count, 1), 0), block_rows) // local_heads
    limit = jnp.where(token < steps, live, 0)
    loads[2].wait()
    position = lax.broadcasted_iota(jnp.int32, (count, cache.shape[0]), 1)
    old = jnp.where(position < limit, scores_of(cache[:, :HEAD_DIM]), -1e30)
    highest = jnp.max(old, axis=-1, keepdims=True)
    new_arrive()
    keyvals = new_ref[...].reshape(n * height, 2 * HEAD_DIM)
    column = lax.broadcasted_iota(jnp.int32, (count, n * height), 1)
    spot = column // height
    owner = lax.rem(spot, chips) * 2 + spot // chips
    kind = lax.rem(column, height)
    reach = jnp.where(token < steps, jnp.where(chosen, n, -1), me)
    from_prefill = (kind == steps) & (owner <= reach)
    from_steps = (kind < steps) & (kind <= token) & (token < steps) & (owner == me)
    new = jnp.where(from_prefill | from_steps, scores_of(keyvals[:, :HEAD_DIM]), -1e30)
    highest = jnp.maximum(highest, jnp.max(new, axis=-1, keepdims=True))
    old = jnp.exp(old - highest)
    new = jnp.exp(new - highest)
    total = jnp.sum(old, axis=-1, keepdims=True) + jnp.sum(new, axis=-1, keepdims=True)
    mixed = jnp.dot(
        old.astype(jnp.bfloat16), cache[:, HEAD_DIM:], preferred_element_type=jnp.float32
    )
    mixed = mixed + jnp.dot(
        new.astype(jnp.bfloat16), keyvals[:, HEAD_DIM:], preferred_element_type=jnp.float32
    )
    mix_from[...] = (mixed / total).reshape(n, block_rows, HEAD_DIM).astype(jnp.bfloat16)
    mix_to[place] = mix_from[place]
    mix_arrive, mix_sent = start_all(mix_from, mix_to, ms.at[0], mr.at[0])
    loads[3].wait()
    mix_arrive()
    flat = mix_to[...].astype(jnp.float32).reshape(n * height, columns).astype(jnp.bfloat16)

    def swap(e):
        return remote(part.at[e, 1 - core], near.at[e], ps.at[e], pr.at[e], sibling)

    def out_across(e, k):
        to = target(k)
        return remote(pair.at[e, to], far.at[e, chip], ss.at[e], sr.at[e], to * 2 + core)

    def out_all(e):
        block = far.at[e, pl.ds(0, chips - 1)]
        return remote(block, block, ss.at[e], sr.at[e], sibling)

    def fold(e):
        swap(e).wait_recv()
        both = part[e, core].astype(jnp.float32) + near[e].astype(jnp.float32)
        pair[e] = both.astype(jnp.bfloat16)
        each(1, chips, lambda k: out_across(e, k).start())
        far[e, chip] = pair[e, chip]

    for e in range(chunks):
        product = jnp.dot(
            flat, wo[:, e * wide : (e + 1) * wide], preferred_element_type=jnp.float32
        )
        part[e] = product.reshape(2, chips, height, wide).astype(jnp.bfloat16)
        swap(e).start()
        if e > 0:
            fold(e - 1)
    fold(chunks - 1)
    for e in range(chunks):
        out_all(e).wait_recv()
        result = jnp.sum(far[e].astype(jnp.float32), axis=0).astype(jnp.bfloat16)
        dec_out[:, e * wide : (e + 1) * wide] = result[:steps]
        pre_out[:, e * wide : (e + 1) * wide] = result[steps:]
    for c in range(chunks):
        across_all(c).wait_send()
        forward(c).wait_send()
        swap(c).wait_send()
        out_all(c).wait_send()
    kv_sent()
    q_sent()
    new_sent()
    mix_sent()


def fused(n, prefill, decode, cache, length, slot, gain, wq, wkv, wo):
    dma = pltpu.SemaphoreType.DMA
    steps, width = decode.shape
    height = steps + 1
    columns = wq.shape[1]
    local_heads = columns // HEAD_DIM
    chunks = 2
    wide = width // chunks
    chips = n // 2
    heads_block = (n, height * local_heads, HEAD_DIM)
    new_block = (n, height, 2 * HEAD_DIM)
    half = (chunks, chips, height, wide)
    narrow = jnp.bfloat16
    hbm = pl.BlockSpec(memory_space=pltpu.HBM)
    return pl.pallas_call(
        functools.partial(fused_kernel, n, steps, local_heads),
        out_shape=(
            jax.ShapeDtypeStruct(prefill.shape, narrow),
            jax.ShapeDtypeStruct(decode.shape, narrow),
        ),
        in_specs=[SMEM, SMEM, VMEM, VMEM, VMEM, hbm, hbm, hbm, hbm],
        out_specs=(VMEM, VMEM),
        scratch_shapes=[
            pltpu.VMEM(cache.shape, narrow),
            pltpu.VMEM(wq.shape, narrow),
            pltpu.VMEM(wkv.shape, narrow),
            pltpu.VMEM(wo.shape, narrow),
            pltpu.VMEM((chunks, 2, chips, height, wide), narrow),
            pltpu.VMEM(heads_block, narrow),
            pltpu.VMEM(heads_block, narrow),
            pltpu.VMEM(new_block, jnp.float32),
            pltpu.VMEM(new_block, jnp.float32),
            pltpu.VMEM(new_block[1:], narrow),
            pltpu.VMEM(new_block, narrow),
            pltpu.VMEM(heads_block, narrow),
            pltpu.VMEM(heads_block, narrow),
            pltpu.VMEM((chunks, 2, chips, height, wide), narrow),
            pltpu.VMEM(half, narrow),
            pltpu.VMEM(half, narrow),
            pltpu.VMEM(half, narrow),
            dma((4,)),
        ]
        + [dma((chunks,))] * 4
        + [dma((1,))] * 8
        + [dma((chunks,))] * 4,
        compiler_params=pltpu.CompilerParams(
            collective_id=4, has_side_effects=True, vmem_limit_bytes=60 * 1024 * 1024
        ),
    )(length, slot, prefill, decode, gain, cache, wq, wkv, wo)


def per_device(
    prefill_rows,
    decode_rows,
    kv_cache,
    slot_lengths,
    prefill_slot,
    norm_gain,
    query_weight,
    keyval_weight,
    output_weight,
):
    n = lax.axis_size("narrow")
    rank = lax.axis_index("narrow")
    steps = decode_rows.shape[1]
    assert decode_rows.shape[0] == 1 and prefill_rows.shape[0] == 1
    height = steps + 1
    width = prefill_rows.shape[1]
    heads = query_weight.shape[0] // HEAD_DIM
    columns = query_weight.shape[1]
    depth = keyval_weight.shape[0]
    if columns % HEAD_DIM == 0 and n % 4 == 0 and depth % HEAD_DIM == 0:
        prefill_out, decode_out = fused(
            n,
            prefill_rows,
            decode_rows[0],
            kv_cache[0],
            slot_lengths,
            prefill_slot,
            norm_gain[None],
            query_weight,
            keyval_weight,
            output_weight,
        )
        return (prefill_out, decode_out[None])
    rows = jnp.concatenate([decode_rows[0], prefill_rows], axis=0)
    normed = gather_rows(n, rows, norm_gain[None])
    flat = normed.reshape(n * height, width)
    queries = jnp.dot(flat, query_weight, preferred_element_type=jnp.float32)
    queries = queries.astype(jnp.bfloat16)
    part = lax.dynamic_slice_in_dim(flat, rank * depth, depth, 1)
    partial = jnp.dot(part, keyval_weight, preferred_element_type=jnp.float32)
    whole_heads = columns % HEAD_DIM == 0
    if whole_heads:
        local_heads = columns // HEAD_DIM
        block = (n, height * local_heads, HEAD_DIM)
    else:
        local_heads = heads
        block = (n, height, columns)
    queries, new = exchange_queries(
        n, queries.reshape(block), partial.reshape(n, height, 2 * HEAD_DIM)
    )
    if not whole_heads:
        queries = queries.transpose(1, 0, 2)
    chosen = rank == prefill_slot[0]
    live = jnp.where(chosen, 0, slot_lengths[0])
    info = jnp.stack([live, chosen.astype(jnp.int32), rank.astype(jnp.int32)])
    mixed = attend(
        steps,
        height,
        local_heads,
        info,
        queries.reshape(height * heads, HEAD_DIM),
        kv_cache[0],
        new.reshape(n * height, 2 * HEAD_DIM),
    )
    if not whole_heads:
        mixed = mixed.reshape(height, n, columns).transpose(1, 0, 2)
    mixed = exchange_mixed(n, mixed.reshape(block))
    partial = jnp.dot(
        mixed.reshape(n * height, columns), output_weight, preferred_element_type=jnp.float32
    )
    out = reduce_rows(n, partial.astype(jnp.bfloat16).reshape(n, height, width))
    return (out[steps:], out[None, :steps])


def solution(mesh):
    in_specs = (
        P(("group", "narrow"), None),
        P(("group", "narrow"), None, None),
        P(("group", "narrow"), None, None),
        P(("group", "narrow")),
        P("group"),
        P(),
        P(None, "narrow"),
        P("narrow", None),
        P("narrow", None),
    )
    out_specs = (P(("group", "narrow"), None), P(("group", "narrow"), None, None))
    return jax.shard_map(
        per_device, mesh=mesh, in_specs=in_specs, out_specs=out_specs, check_vma=False
    )
```
